512 devices in a mesh: ctx: 64 (over z, y_hi, core), tp: 8 (over x, y_lo).
Axes of the slice: x: 4, y: 4 (y_hi: 2, y_lo: 2; y = y_hi * 2 + y_lo), z: 16, core: 2. Of those that a mesh axis runs over, the one named last changes fastest.
Arguments:
- block_queries: bfloat16 [8192, 8192], P('ctx', 'tp'), may hold values from -200 to 200
- block_keys: bfloat16 [8192, 1024], P('ctx', 'tp'), may hold values from -6 to 6
- block_values: bfloat16 [8192, 1024], P('ctx', 'tp'), may hold values from -6 to 6
- block_lengths: int32 [64], replicated, may hold values from 1 to 128, 6144 in all
- row_queries: bfloat16 [128, 8192], P(None, 'tp'), may hold values from -200 to 200
- row_keys: bfloat16 [128, 1024], P(None, 'tp'), may hold values from -6 to 6
- row_values: bfloat16 [128, 1024], P(None, 'tp'), may hold values from -6 to 6
- out_weight: bfloat16 [8192, 8192], P('tp', 'ctx'), may hold values from -0.0625 to 0.0625
Outputs:
- block_attention: bfloat16 [8192, 8192], P('ctx', 'tp')
- row_output: float32 [128, 8192], P(None, 'ctx')
The draws below stay inside these ranges and needn't reach their ends.
All inputs are finite; a program needn't handle non-finite values.
Results may differ from the reference program's by a relative error of at most 0.0065.
Values may be sent and summed in bfloat16 or wider, within the bound.
No kernel may reach another device: no remote copies, remote signals or barrier semaphores. Data moves between devices by JAX's collectives and lax.ppermute only.
A program may use at most 192 MiB of HBM per device.

```python
import math
import jax
import jax.numpy as jnp
import numpy as np
from jax import lax

D = 8192
HEADS = 64
KV_HEADS = 8
HD = 128
BLK = 128
QROWS = 128
GROUP = 8
DOC = 8192
N_CTX = 64


def base_keys(key, count, salt):
    inner = jax.random.fold_in(key, salt)
    return jnp.clip(jax.random.normal(inner, (count, KV_HEADS * HD), jnp.float32), -6.0, 6.0)


def shaped_keys(key, count, salt):
    keys = base_keys(key, count, salt)
    return keys.astype(jnp.bfloat16)


def shaped_queries(key, count, fresh):
    queries = jnp.clip(2.5 * jax.random.normal(fresh, (count, HEADS * HD), jnp.float32), -15.0, 15.0)
    return queries.astype(jnp.bfloat16)


def draw_block_keys(key, part):
    return shaped_keys(key, DOC, 101)


def draw_block_queries(key, part):
    fresh = jax.random.fold_in(key, 3)
    return shaped_queries(key, DOC, fresh)


def draw_row_keys(key, part):
    return shaped_keys(key, QROWS, 202)


def draw_row_queries(key, part):
    fresh = jax.random.fold_in(key, 4)
    return shaped_queries(key, QROWS, fresh)


def block_levels(stream_key, extent, split, smallest, largest):
    level, own = 1.0, jax.random.fold_in(stream_key, 6)
    for dim, parts in split:
        heights = jnp.exp(jax.random.uniform(jax.random.fold_in(own, dim), (parts,), jnp.float32, smallest / len(split), largest / len(split)))
        level = level * jnp.repeat(heights, extent[dim] // parts).reshape([-1 if axis == dim else 1 for axis in range(len(extent))])
    return level


def profile(count, total, most, slope):
    loads = [(1 << 20) // math.isqrt(standing ** slope) + 1 for standing in range(2, count + 1)]
    spare, counts = total - most - (count - 1), [1] * (count - 1)
    while spare > 0:
        candidates = [i for i in range(count - 1) if counts[i] < most]
        mass, left = sum([loads[i] for i in candidates]), spare
        for i in candidates:
            extra = min(most - counts[i], max(1, left * loads[i] // mass), spare)
            counts[i] = counts[i] + extra
            spare = spare - extra
    return np.array([most] + counts)


def ragged(rng, amount, total, limit, slope):
    if amount == 2:
        one = jax.random.randint(rng, (), max(1, total - limit), min(limit, total - 1) + 1)
        return jnp.stack([one, total - one])
    lengths = jnp.asarray(profile(amount, total, limit, slope), jnp.int32)
    couples = (amount - 1) // 2
    donor, sink = lengths[1:1 + 2 * couples:2], lengths[2:2 + 2 * couples:2]
    slack = jnp.minimum(donor - 1, limit - sink)
    passed = jax.random.randint(jax.random.fold_in(rng, 1), (couples,), 0, 1 << 20) % (slack + 1)
    lengths = lengths.at[1:1 + 2 * couples:2].set(donor - passed).at[2:2 + 2 * couples:2].set(sink + passed)
    return lengths[jax.random.permutation(jax.random.fold_in(rng, 2), amount)]


def scatter_about(own_key, extent, deviation, reach, shards=(), kind=jnp.bfloat16):
    result = jax.random.normal(own_key, extent, jnp.float32) * deviation
    if len(shards) > 0:
        result = block_levels(own_key, extent, shards, -0.22, 0.18) * result
    return jnp.clip(result, min=-reach, max=reach).astype(kind)


def setup_inputs(seed: int = 0) -> dict:
    streams_of = jax.random.split(jax.random.key(seed), 9)
    return {
        "block_queries": draw_block_queries(jax.random.fold_in(streams_of[8], 71), 0),
        "block_keys": draw_block_keys(jax.random.fold_in(streams_of[8], 71), 0),
        "block_values": scatter_about(streams_of[2], (DOC, KV_HEADS * HD), 1.0, 6.0, ((0, 64), (1, 8))),
        "block_lengths": ragged(streams_of[3], N_CTX, BLK * N_CTX * 3 // 4, BLK, 2).astype(jnp.int32),
        "row_queries": draw_row_queries(jax.random.fold_in(streams_of[8], 71), 0),
        "row_keys": draw_row_keys(jax.random.fold_in(streams_of[8], 71), 0),
        "row_values": scatter_about(streams_of[6], (QROWS, KV_HEADS * HD), 1.0, 6.0, ((1, 8),)),
        "out_weight": scatter_about(streams_of[7], (HEADS * HD, D), (HEADS * HD) ** -0.5, 0.0625, ((0, 8), (1, 64))),
    }


NEG = -1.0e30


def softmax_parts(scores, mask, values):
    scores = jnp.where(mask, scores, NEG)
    top = jnp.max(scores, axis=-1)
    expo = jnp.where(mask, jnp.exp(scores - top[..., None]), 0.0)
    total = jnp.sum(expo, axis=-1)
    weights = expo.astype(jnp.bfloat16).astype(jnp.float32)
    summed = jnp.einsum('kgij,jkd->kgid', weights, values.astype(jnp.float32))
    return top, total, summed


def reference(block_queries, block_keys, block_values, block_lengths, row_queries, row_keys, row_values, out_weight):
    scale = HD ** -0.5
    queries = block_queries.reshape(N_CTX, BLK, KV_HEADS, GROUP, HD)
    keys = block_keys.reshape(N_CTX, BLK, KV_HEADS, HD)
    values = block_values.reshape(N_CTX, BLK, KV_HEADS, HD)
    anchor_len = block_lengths[0]
    slots = jnp.arange(2 * BLK, dtype=jnp.int32)
    rows = jnp.arange(BLK, dtype=jnp.int32)

    def one_block(index):
        length = block_lengths[index]
        both_k = jnp.concatenate([keys[0], keys[index]], axis=0)
        both_v = jnp.concatenate([values[0], values[index]], axis=0)
        anchor_ok = (slots < BLK) & (slots < anchor_len) & (index > 0)
        own_ok = (slots[None, :] >= BLK) & (slots[None, :] - BLK <= rows[:, None]) & (slots[None, :] - BLK < length)
        mask = anchor_ok[None, :] | own_ok
        scores = jnp.einsum('ikgd,jkd->kgij', queries[index].astype(jnp.float32), both_k.astype(jnp.float32)) * scale
        top, total, summed = softmax_parts(scores, mask, both_v)
        out = summed / total[..., None]
        return jnp.transpose(out, (2, 0, 1, 3)).reshape(BLK, HEADS * HD).astype(jnp.bfloat16)

    block_attention = lax.map(one_block, jnp.arange(N_CTX, dtype=jnp.int32)).reshape(DOC, HEADS * HD)

    row_q = row_queries.reshape(QROWS, KV_HEADS, GROUP, HD).astype(jnp.float32)
    own_k = row_keys.reshape(QROWS, KV_HEADS, HD)
    own_v = row_values.reshape(QROWS, KV_HEADS, HD)
    qpos = jnp.arange(QROWS, dtype=jnp.int32)
    own_mask = qpos[None, :] <= qpos[:, None]
    own_scores = jnp.einsum('ikgd,jkd->kgij', row_q, own_k.astype(jnp.float32)) * scale
    start = softmax_parts(own_scores, own_mask, own_v)

    def step(carry, index):
        top_a, total_a, sum_a = carry
        length = block_lengths[index]
        mask = jnp.broadcast_to((rows < length)[None, :], (QROWS, BLK))
        scores = jnp.einsum('ikgd,jkd->kgij', row_q, keys[index].astype(jnp.float32)) * scale
        top_b, total_b, sum_b = softmax_parts(scores, mask, values[index])
        top = jnp.maximum(top_a, top_b)
        fa = jnp.exp(top_a - top)
        fb = jnp.exp(top_b - top)
        return (top, total_a * fa + total_b * fb, sum_a * fa[..., None] + sum_b * fb[..., None]), None

    final, unused = lax.scan(step, start, jnp.arange(N_CTX, dtype=jnp.int32))
    attn = final[2] / final[1][..., None]
    attn = jnp.transpose(attn, (2, 0, 1, 3)).reshape(QROWS, HEADS * HD).astype(jnp.bfloat16)
    row_output = jnp.dot(attn, out_weight, preferred_element_type=jnp.float32)
    return block_attention, row_output
```

```python
import jax
import jax.numpy as jnp
from jax import lax
from jax.experimental import pallas as pl
from jax.experimental.pallas import tpu as pltpu
from jax.sharding import Mesh, PartitionSpec as P

HD = 128
BLK = 128
HEADS = 8
SCALE = HD ** (-0.5)
NEG = -1e30
CTX = ("zh", "zl", "yh", "core")
GROUP = ("zl", "yh")
O = 64
MSG = 96
LAST = 80
F32, BF16 = jnp.float32, jnp.bfloat16


def dot_nt(a, b):
    return lax.dot_general(a, b, (((1,), (1,)), ((), ())), preferred_element_type=F32)


def dot_tn(a, b):
    return lax.dot_general(a, b, (((0,), (0,)), ((), ())), preferred_element_type=F32)


def rows_of(shape, dim):
    return lax.broadcasted_iota(jnp.int32, shape, dim)


def split(x):
    high = x.astype(BF16).astype(F32)
    return high, (x - high).astype(BF16).astype(F32)


def position():
    zh, zl, yh, core = (lax.axis_index(a) for a in CTX)
    return zh, zl, yh, core


def statistics(m_high, m_low, total):
    t_high, t_low = split(total)
    r = rows_of((16, 128), 0)
    zero = jnp.zeros((16, 128), F32)
    out = jnp.where(r == 0, m_high, zero)
    out = jnp.where(r == 1, m_low, out)
    out = jnp.where(r == 2, t_high, out)
    return jnp.where(r == 3, t_low, out).astype(BF16)


def column_softmax(scores, mask):
    scores = jnp.where(mask, scores, NEG)
    high, low = split(jnp.max(scores, axis=0, keepdims=True))
    e = jnp.where(mask, jnp.exp(scores - (high + low)), 0.0)
    return high, low, e


def own_kernel(q_ref, k_ref, v_ref, out_ref, scratch):
    zh, zl, yh, core = position()
    q = q_ref[:, pl.ds(pl.multiple_of((core * 4 + zl) * HD, HD), HD)]
    s = dot_nt(k_ref[...], q) * SCALE
    mask = rows_of(s.shape, 0) <= rows_of(s.shape, 1)
    high, low, e = column_softmax(s, mask)
    scratch[...] = dot_tn(v_ref[...], e.astype(BF16))
    out_ref[0:O, :] = scratch[pl.ds(pl.multiple_of(yh * O, O), O), :]
    r = rows_of((8, 128), 0)
    out_ref[O : O + 8, :] = jnp.where(r == 0, high + low, jnp.sum(e, axis=0, keepdims=True))


def partial_kernel(len_ref, q_ref, k_ref, v_ref, sib_ref, out_ref):
    zh, zl, yh, core = position()
    ctx = ((zh * 4 + zl) * 2 + yh) * 2 + core
    keys = jnp.concatenate([k_ref[...], sib_ref[0:BLK, :]], axis=0)
    values = jnp.concatenate([v_ref[...], sib_ref[BLK:, :]], axis=0)
    slot = rows_of((2 * BLK, 128), 0)
    mine, other = len_ref[ctx], len_ref[ctx + 1 - 2 * core]
    mask = (slot < mine) | ((slot >= BLK) & (slot < BLK + other))
    for i in range(4):
        q = q_ref[:, pl.ds(pl.multiple_of((core * 4 + i) * HD, HD), HD)]
        s = dot_nt(keys, q) * SCALE
        high, low, e = column_softmax(s, mask)
        stats = statistics(high, low, jnp.sum(e, axis=0, keepdims=True))
        o = dot_tn(values, e.astype(BF16)).astype(BF16)
        for half in range(2):
            out_ref[2 * i + half, 0:O, :] = o[half * O : (half + 1) * O, :]
            out_ref[2 * i + half, O : O + 16, :] = stats

    @pl.when(core == 0)
    def _():
        for j in range(8):
            out_ref[j, O + 16 : MSG, :] = k_ref[16 * j : 16 * j + 16, :]

    @pl.when(core == 1)
    def _():
        for j in range(8):
            out_ref[j, O + 16 : MSG, :] = sib_ref[BLK + 16 * j : BLK + 16 * j + 16, :]


def combine(ref, count, more=()):
    ms, ts, os = [], [], []
    for i in range(count):
        st = ref[i, O : O + 16, :].astype(F32)
        ms.append((st[0:1], st[1:2]))
        ts.append(st[2:3] + st[3:4])
        os.append(ref[i, 0:O, :].astype(F32))
    high, low = ms[0]
    for h, l in ms[1:]:
        better = h + l > high + low
        high, low = jnp.where(better, h, high), jnp.where(better, l, low)
    top = high + low
    for m, _, _ in more:
        top = jnp.maximum(top, m)
    total = jnp.zeros_like(top)
    summed = jnp.zeros((O, 128), F32)
    for (h, l), t, o in zip(ms, ts, os):
        w = jnp.exp(h + l - top)
        total, summed = total + t * w, summed + o * w
    for m, t, o in more:
        w = jnp.exp(m - top)
        total, summed = total + t * w, summed + o * w
    return high, low, total, summed


def group_kernel(in_ref, out_ref):
    high, low, total, summed = combine(in_ref, 8)
    stats = statistics(high, low, total)
    o = summed.astype(BF16)
    for i in range(4):
        out_ref[i, 0:O, :] = o
        out_ref[i, O : O + 16, :] = stats
        out_ref[i, O + 16 : MSG, :] = in_ref[0, O + 16 : MSG, :]


def final_kernel(in_ref, own_ref, out_ref):
    own = (own_ref[O : O + 1, :], own_ref[O + 1 : O + 2, :], own_ref[0:O, :])
    _, _, total, summed = combine(in_ref, 4, (own,))
    attn = (summed / total).astype(BF16)
    for i in range(8):
        out_ref[i, 0:O, :] = attn
        out_ref[i, O:LAST, :] = in_ref[0, O + 16 : MSG, :]


def project_kernel(mine_ref, sib_ref, w_ref, out_ref):
    zh, zl, yh, core = position()
    def four(ref, which):
        a = jnp.concatenate([ref[j, 0:O, :] for j in range(8)], axis=0)
        return dot_tn(a, w_ref[pl.ds(pl.multiple_of(which * 4 * HD, 4 * HD), 4 * HD), :])

    out = four(mine_ref, core) + four(sib_ref, 1 - core)
    for i in range(8):
        out_ref[i, :, :] = out


def block_kernel(len_ref, q_ref, k_ref, v_ref, mine_ref, sib_ref, out_ref, anchor):
    zh, zl, yh, core = position()
    ctx = ((zh * 4 + zl) * 2 + yh) * 2 + core
    for j in range(8):
        anchor[core, 16 * j : 16 * j + 16, :] = mine_ref[j, O:LAST, :]
        anchor[1 - core, 16 * j : 16 * j + 16, :] = sib_ref[j, O:LAST, :]
    keys = jnp.concatenate([anchor[0], k_ref[...]], axis=0)
    values = jnp.concatenate([anchor[1], v_ref[...]], axis=0)
    length = len_ref[ctx]
    first = jnp.where(ctx > 0, len_ref[0], 0)
    slot, row = rows_of((BLK, 2 * BLK), 1), rows_of((BLK, 2 * BLK), 0)
    mask = (slot < jnp.minimum(first, BLK)) | (
        (slot >= BLK) & (slot - BLK <= row) & (slot - BLK < length)
    )
    for h in range(HEADS):
        s = dot_nt(q_ref[:, h * HD : (h + 1) * HD], keys) * SCALE
        s = jnp.where(mask, s, NEG)
        e = jnp.where(mask, jnp.exp(s - jnp.max(s, axis=1, keepdims=True)), 0.0)
        total = jnp.sum(e, axis=1, keepdims=True)
        o = jnp.dot(e.astype(BF16), values, preferred_element_type=F32)
        out_ref[:, h * HD : (h + 1) * HD] = (o / total).astype(BF16)


SMEM = pl.BlockSpec(memory_space=pltpu.SMEM)
VMEM = pl.BlockSpec(memory_space=pltpu.VMEM)


def call(kernel, shape, dtype, *args, lengths=False, scratch=(), flops=0):
    specs = ([SMEM] if lengths else []) + [VMEM] * (len(args) - (1 if lengths else 0))
    moved = sum(a.size * a.dtype.itemsize for a in args)
    return pl.pallas_call(
        kernel,
        out_shape=jax.ShapeDtypeStruct(shape, dtype),
        in_specs=specs,
        out_specs=VMEM,
        scratch_shapes=scratch,
        cost_estimate=pl.CostEstimate(flops=flops, bytes_accessed=moved, transcendentals=0),
    )(*args)


def exchange(x, axes):
    return lax.all_to_all(x, axes, 0, 0, tiled=True)


SWAP = [(0, 1), (1, 0)]


def per_device(bq, bk, bv, lengths, rq, rk, rv, w):
    sib = lax.ppermute(jnp.concatenate([bk, bv], axis=0), "core", SWAP)
    own = call(own_kernel, (O + 8, 128), F32, rq, rk, rv, scratch=[pltpu.VMEM((HD, 128), F32)])
    parts = call(partial_kernel, (8, MSG, 128), BF16, lengths, rq, bk, bv, sib, lengths=True)
    parts = exchange(parts, GROUP)
    grouped = call(group_kernel, (4, MSG, 128), BF16, parts)
    grouped = exchange(grouped, "zh")
    attn = call(final_kernel, (8, LAST, 128), BF16, grouped, own)
    attn = exchange(attn, GROUP)
    attn_sib = lax.ppermute(attn, "core", SWAP)
    partial = call(project_kernel, (8, 128, 128), F32, attn, attn_sib, w)
    partial = exchange(partial, "tp")
    row_output = jnp.sum(partial, axis=0)
    block_attention = call(
        block_kernel, bq.shape, BF16, lengths, bq, bk, bv, attn, attn_sib,
        lengths=True, scratch=[pltpu.VMEM((2, BLK, HD), BF16)],
    )
    return block_attention, row_output


def solution(mesh):
    fine = Mesh(mesh.devices.reshape(4, 4, 2, 2, 8), CTX + ("tp",))
    return jax.shard_map(
        per_device,
        mesh=fine,
        in_specs=(
            P(CTX, "tp"),
            P(CTX, "tp"),
            P(CTX, "tp"),
            P(),
            P(None, "tp"),
            P(None, "tp"),
            P(None, "tp"),
            P("tp", CTX),
        ),
        out_specs=(P(CTX, "tp"), P(None, CTX)),
        check_vma=False,
    )
```

```python
import jax
import jax.numpy as jnp
from jax import lax
from jax.experimental import pallas as pl
from jax.experimental.pallas import tpu as pltpu
from jax.sharding import Mesh, PartitionSpec as P

HD = 128
BLK = 128
HEADS = 8
SCALE = HD ** (-0.5)
NEG = -1e30
CTX = ("zh", "zl", "yh", "core")
GROUP = ("zl", "yh")
O = 64
MSG = 96
LAST = 80
F32, BF16 = jnp.float32, jnp.bfloat16


def dot_nt(a, b):
    return lax.dot_general(a, b, (((1,), (1,)), ((), ())), preferred_element_type=F32)


def dot_tn(a, b):
    return lax.dot_general(a, b, (((0,), (0,)), ((), ())), preferred_element_type=F32)


def rows_of(shape, dim):
    return lax.broadcasted_iota(jnp.int32, shape, dim)


def split(x):
    high = x.astype(BF16).astype(F32)
    return high, (x - high).astype(BF16).astype(F32)


def position():
    zh, zl, yh, core = (lax.axis_index(a) for a in CTX)
    return zh, zl, yh, core


def statistics(m_high, m_low, total):
    t_high, t_low = split(total)
    r = rows_of((16, 128), 0)
    zero = jnp.zeros((16, 128), F32)
    out = jnp.where(r == 0, m_high, zero)
    out = jnp.where(r == 1, m_low, out)
    out = jnp.where(r == 2, t_high, out)
    return jnp.where(r == 3, t_low, out).astype(BF16)


def column_softmax(scores, mask):
    scores = jnp.where(mask, scores, NEG)
    high, low = split(jnp.max(scores, axis=0, keepdims=True))
    e = jnp.where(mask, jnp.exp(scores - (high + low)), 0.0)
    return high, low, e


def own_kernel(q_ref, k_ref, v_ref, out_ref, scratch):
    zh, zl, yh, core = position()
    q = q_ref[:, pl.ds(pl.multiple_of((core * 4 + zl) * HD, HD), HD)]
    s = dot_nt(k_ref[...], q) * SCALE
    mask = rows_of(s.shape, 0) <= rows_of(s.shape, 1)
    high, low, e = column_softmax(s, mask)
    scratch[...] = dot_tn(v_ref[...], e.astype(BF16))
    out_ref[0:O, :] = scratch[pl.ds(pl.multiple_of(yh * O, O), O), :]
    r = rows_of((8, 128), 0)
    out_ref[O : O + 8, :] = jnp.where(r == 0, high + low, jnp.sum(e, axis=0, keepdims=True))


def partial_kernel(len_ref, q_ref, k_ref, v_ref, sib_ref, out_ref):
    zh, zl, yh, core = position()
    ctx = ((zh * 4 + zl) * 2 + yh) * 2 + core
    keys = jnp.concatenate([k_ref[...], sib_ref[0:BLK, :]], axis=0)
    values = jnp.concatenate([v_ref[...], sib_ref[BLK:, :]], axis=0)
    slot = rows_of((2 * BLK, 128), 0)
    mine, other = len_ref[ctx], len_ref[ctx + 1 - 2 * core]
    mask = (slot < mine) | ((slot >= BLK) & (slot < BLK + other))
    for i in range(4):
        q = q_ref[:, pl.ds(pl.multiple_of((core * 4 + i) * HD, HD), HD)]
        s = dot_nt(keys, q) * SCALE
        high, low, e = column_softmax(s, mask)
        stats = statistics(high, low, jnp.sum(e, axis=0, keepdims=True))
        o = dot_tn(values, e.astype(BF16)).astype(BF16)
        for half in range(2):
            out_ref[2 * i + half, 0:O, :] = o[half * O : (half + 1) * O, :]
            out_ref[2 * i + half, O : O + 16, :] = stats

    @pl.when(core == 0)
    def _():
        for j in range(8):
            out_ref[j, O + 16 : MSG, :] = k_ref[16 * j : 16 * j + 16, :]

    @pl.when(core == 1)
    def _():
        for j in range(8):
            out_ref[j, O + 16 : MSG, :] = sib_ref[BLK + 16 * j : BLK + 16 * j + 16, :]


def combine(ref, count, more=()):
    ms, ts, os = [], [], []
    for i in range(count):
        st = ref[i, O : O + 16, :].astype(F32)
        ms.append((st[0:1], st[1:2]))
        ts.append(st[2:3] + st[3:4])
        os.append(ref[i, 0:O, :].astype(F32))
    high, low = ms[0]
    for h, l in ms[1:]:
        better = h + l > high + low
        high, low = jnp.where(better, h, high), jnp.where(better, l, low)
    top = high + low
    for m, _, _ in more:
        top = jnp.maximum(top, m)
    total = jnp.zeros_like(top)
    summed = jnp.zeros((O, 128), F32)
    for (h, l), t, o in zip(ms, ts, os):
        w = jnp.exp(h + l - top)
        total, summed = total + t * w, summed + o * w
    for m, t, o in more:
        w = jnp.exp(m - top)
        total, summed = total + t * w, summed + o * w
    return high, low, total, summed


def group_kernel(in_ref, out_ref):
    high, low, total, summed = combine(in_ref, 8)
    stats = statistics(high, low, total)
    o = summed.astype(BF16)
    for i in range(4):
        out_ref[i, 0:O, :] = o
        out_ref[i, O : O + 16, :] = stats
        out_ref[i, O + 16 : MSG, :] = in_ref[0, O + 16 : MSG, :]


def final_kernel(in_ref, own_ref, out_ref):
    own = (own_ref[O : O + 1, :], own_ref[O + 1 : O + 2, :], own_ref[0:O, :])
    _, _, total, summed = combine(in_ref, 4, (own,))
    attn = (summed / total).astype(BF16)
    for i in range(8):
        out_ref[i, 0:O, :] = attn
        out_ref[i, O:LAST, :] = in_ref[2, O + 16 : MSG, :]


def project_kernel(mine_ref, sib_ref, w_ref, out_ref):
    zh, zl, yh, core = position()
    def four(ref, which):
        a = jnp.concatenate([ref[j, 0:O, :] for j in range(8)], axis=0)
        return dot_tn(a, w_ref[pl.ds(pl.multiple_of(which * 4 * HD, 4 * HD), 4 * HD), :])

    out = four(mine_ref, core) + four(sib_ref, 1 - core)
    for i in range(8):
        out_ref[i, :, :] = out


def block_kernel(len_ref, q_ref, k_ref, v_ref, mine_ref, sib_ref, out_ref, anchor):
    zh, zl, yh, core = position()
    ctx = ((zh * 4 + zl) * 2 + yh) * 2 + core
    for j in range(8):
        anchor[core, 16 * j : 16 * j + 16, :] = mine_ref[j, O:LAST, :]
        anchor[1 - core, 16 * j : 16 * j + 16, :] = sib_ref[j, O:LAST, :]
    keys = jnp.concatenate([anchor[0], k_ref[...]], axis=0)
    values = jnp.concatenate([anchor[1], v_ref[...]], axis=0)
    length = len_ref[ctx]
    first = jnp.where(ctx > 0, len_ref[0], 0)
    slot, row = rows_of((BLK, 2 * BLK), 1), rows_of((BLK, 2 * BLK), 0)
    mask = (slot < jnp.minimum(first, BLK)) | (
        (slot >= BLK) & (slot - BLK <= row) & (slot - BLK < length)
    )
    for h in range(HEADS):
        s = dot_nt(q_ref[:, h * HD : (h + 1) * HD], keys) * SCALE
        s = jnp.where(mask, s, NEG)
        e = jnp.where(mask, jnp.exp(s - jnp.max(s, axis=1, keepdims=True)), 0.0)
        total = jnp.sum(e, axis=1, keepdims=True)
        o = jnp.dot(e.astype(BF16), values, preferred_element_type=F32)
        out_ref[:, h * HD : (h + 1) * HD] = (o / total).astype(BF16)


SMEM = pl.BlockSpec(memory_space=pltpu.SMEM)
VMEM = pl.BlockSpec(memory_space=pltpu.VMEM)


def call(kernel, shape, dtype, *args, lengths=False, scratch=(), flops=0):
    specs = ([SMEM] if lengths else []) + [VMEM] * (len(args) - (1 if lengths else 0))
    moved = sum(a.size * a.dtype.itemsize for a in args)
    return pl.pallas_call(
        kernel,
        out_shape=jax.ShapeDtypeStruct(shape, dtype),
        in_specs=specs,
        out_specs=VMEM,
        scratch_shapes=scratch,
        compiler_params=pltpu.CompilerParams(vmem_limit_bytes=6 << 20),
        cost_estimate=pl.CostEstimate(flops=flops, bytes_accessed=moved, transcendentals=0),
    )(*args)


def exchange(x, axes, order=None):
    return lax.all_to_all(x, axes, 0, 0, axis_index_groups=order, tiled=True)


SWAP = [(0, 1), (1, 0)]


def per_device(bq, bk, bv, lengths, rq, rk, rv, w):
    sib = lax.ppermute(jnp.concatenate([bk, bv], axis=0), "core", SWAP)
    own = call(own_kernel, (O + 8, 128), F32, rq, rk, rv, scratch=[pltpu.VMEM((HD, 128), F32)])
    parts = call(partial_kernel, (8, MSG, 128), BF16, lengths, rq, bk, bv, sib, lengths=True)
    parts = exchange(parts, GROUP)
    grouped = call(group_kernel, (4, MSG, 128), BF16, parts)
    grouped = exchange(grouped, "zh", [[2, 3, 0, 1]])
    attn = call(final_kernel, (8, LAST, 128), BF16, grouped, own)
    attn = exchange(attn, GROUP)
    attn_sib = lax.ppermute(attn, "core", SWAP)
    partial = call(project_kernel, (8, 128, 128), F32, attn, attn_sib, w)
    partial = exchange(partial, "tp")
    row_output = jnp.sum(partial, axis=0)
    block_attention = call(
        block_kernel, bq.shape, BF16, lengths, bq, bk, bv, attn, attn_sib,
        lengths=True, scratch=[pltpu.VMEM((2, BLK, HD), BF16)],
    )
    return block_attention, row_output


def solution(mesh):
    fine = Mesh(mesh.devices.reshape(4, 4, 2, 2, 8), CTX + ("tp",))
    return jax.shard_map(
        per_device,
        mesh=fine,
        in_specs=(
            P(CTX, "tp"),
            P(CTX, "tp"),
            P(CTX, "tp"),
            P(),
            P(None, "tp"),
            P(None, "tp"),
            P(None, "tp"),
            P("tp", CTX),
        ),
        out_specs=(P(CTX, "tp"), P(None, CTX)),
        check_vma=False,
    )
```

```python
import jax
import jax.numpy as jnp
from jax import lax
from jax.experimental import pallas as pl
from jax.experimental.pallas import tpu as pltpu
from jax.sharding import Mesh, PartitionSpec as P

HD = 128
BLK = 128
HEADS = 8
SCALE = HD ** (-0.5)
NEG = -1e30
CTX = ("zh", "zl", "yh", "core")
FAR = (2, 3, 0, 1)
NEAR = (2, 3, 0, 1, 4, 5, 6, 7)
SLOT = tuple(NEAR.index(j) for j in range(8))
GROUP = ("zl", "yh")
O = 64
MSG = 96
LAST = 80
F32, BF16 = jnp.float32, jnp.bfloat16


def dot_nt(a, b):
    return lax.dot_general(a, b, (((1,), (1,)), ((), ())), preferred_element_type=F32)


def dot_tn(a, b):
    return lax.dot_general(a, b, (((0,), (0,)), ((), ())), preferred_element_type=F32)


def rows_of(shape, dim):
    return lax.broadcasted_iota(jnp.int32, shape, dim)


def split(x):
    high = x.astype(BF16).astype(F32)
    return high, (x - high).astype(BF16).astype(F32)


def position():
    zh, zl, yh, core = (lax.axis_index(a) for a in CTX)
    return zh, zl, yh, core


def statistics(m_high, m_low, total):
    t_high, t_low = split(total)
    r = rows_of((16, total.shape[1]), 0)
    zero = jnp.zeros(r.shape, F32)
    out = jnp.where(r == 0, m_high, zero)
    out = jnp.where(r == 1, m_low, out)
    out = jnp.where(r == 2, t_high, out)
    return jnp.where(r == 3, t_low, out).astype(BF16)


def column_softmax(scores, mask):
    scores = jnp.where(mask, scores, NEG)
    high, low = split(jnp.max(scores, axis=0, keepdims=True))
    e = jnp.where(mask, jnp.exp(scores - (high + low)), 0.0)
    return high, low, e


def heads_softmax(scores, mask):
    high, low, e = column_softmax(scores, mask)
    return high, low, jnp.sum(e, axis=0, keepdims=True), e.astype(BF16)


def load_kernel(k_ref, v_ref, q_ref, kv_ref, q4_ref, sem):
    core = lax.axis_index("core")
    copies = [
        pltpu.make_async_copy(k_ref, kv_ref.at[0:BLK], sem.at[0]),
        pltpu.make_async_copy(v_ref, kv_ref.at[BLK : 2 * BLK], sem.at[1]),
    ]
    for i in range(4):
        columns = pl.ds(pl.multiple_of((core * 4 + i) * HD, HD), HD)
        rows = slice(i * BLK, (i + 1) * BLK)
        copies.append(pltpu.make_async_copy(q_ref.at[:, columns], q4_ref.at[rows], sem.at[2 + i]))
    for c in copies:
        c.start()
    for c in copies:
        c.wait()


def early_kernel(len_ref, q_ref, kv_ref, rk_ref, rv_ref, own_ref, o_ref, st_ref, scratch):
    zh, zl, yh, core = position()
    ctx = ((zh * 4 + zl) * 2 + yh) * 2 + core
    s = dot_nt(kv_ref[0:BLK, :], q_ref[...]) * SCALE
    own = dot_nt(rk_ref[...], q_ref[pl.ds(pl.multiple_of(zl * HD, HD), HD), :]) * SCALE
    high, low, total, e = heads_softmax(s, rows_of(s.shape, 0) < len_ref[ctx])
    o_ref[...] = dot_tn(kv_ref[BLK:, :], e)
    r = rows_of((8, 512), 0)
    st_ref[...] = jnp.where(r == 0, high, jnp.where(r == 1, low, total))
    high, low, total, e = heads_softmax(own, rows_of(own.shape, 0) <= rows_of(own.shape, 1))
    scratch[...] = dot_tn(rv_ref[...], e)
    own_ref[0:O, :] = scratch[pl.ds(pl.multiple_of(yh * O, O), O), :]
    r = rows_of((8, 128), 0)
    own_ref[O : O + 8, :] = jnp.where(r == 0, high + low, total)


def partial_kernel(len_ref, q_ref, kv_ref, sib_ref, own_ref, o_ref, st_ref, out_ref):
    zh, zl, yh, core = position()
    ctx = ((zh * 4 + zl) * 2 + yh) * 2 + core
    s = dot_nt(sib_ref[0:BLK, :], q_ref[...]) * SCALE
    high, low, total, e = heads_softmax(s, rows_of(s.shape, 0) < len_ref[ctx + 1 - 2 * core])
    o = dot_tn(sib_ref[BLK:, :], e)
    high_a, low_a, total_a = st_ref[0:1, :], st_ref[1:2, :], st_ref[2:3, :]
    better = high_a + low_a > high + low
    top_high, top_low = jnp.where(better, high_a, high), jnp.where(better, low_a, low)
    top = top_high + top_low
    wa, wb = jnp.exp(high_a + low_a - top), jnp.exp(high + low - top)
    stats = statistics(top_high, top_low, total_a * wa + total * wb)
    o = (o_ref[...] * wa + o * wb).astype(BF16)
    for j in range(8):
        cols = slice(j // 2 * HD, (j // 2 + 1) * HD)
        out_ref[SLOT[j], 0:O, :] = o[j % 2 * O : (j % 2 + 1) * O, cols]
        out_ref[SLOT[j], O : O + 16, :] = stats[:, cols]

    @pl.when(core == 0)
    def _():
        for j in range(8):
            out_ref[SLOT[j], O + 16 : MSG, :] = kv_ref[16 * j : 16 * j + 16, :]

    @pl.when(core == 1)
    def _():
        for j in range(8):
            out_ref[SLOT[j], O + 16 : MSG, :] = sib_ref[BLK + 16 * j : BLK + 16 * j + 16, :]


def combine(ref, count, more=()):
    ms, ts, os = [], [], []
    for i in range(count):
        st = ref[i, O : O + 16, :].astype(F32)
        ms.append((st[0:1], st[1:2]))
        ts.append(st[2:3] + st[3:4])
        os.append(ref[i, 0:O, :].astype(F32))
    high, low = ms[0]
    for h, l in ms[1:]:
        better = h + l > high + low
        high, low = jnp.where(better, h, high), jnp.where(better, l, low)
    top = high + low
    for m, _, _ in more:
        top = jnp.maximum(top, m)
    total = jnp.zeros_like(top)
    summed = jnp.zeros((O, 128), F32)
    for (h, l), t, o in zip(ms, ts, os):
        w = jnp.exp(h + l - top)
        total, summed = total + t * w, summed + o * w
    for m, t, o in more:
        w = jnp.exp(m - top)
        total, summed = total + t * w, summed + o * w
    return high, low, total, summed


def group_kernel(in_ref, out_ref):
    high, low, total, summed = combine(in_ref, 8)
    stats = statistics(high, low, total)
    o = summed.astype(BF16)
    for i in range(4):
        out_ref[i, 0:O, :] = o
        out_ref[i, O : O + 16, :] = stats
        out_ref[i, O + 16 : MSG, :] = in_ref[SLOT[0], O + 16 : MSG, :]


def final_kernel(in_ref, own_ref, out_ref):
    own = (own_ref[O : O + 1, :], own_ref[O + 1 : O + 2, :], own_ref[0:O, :])
    _, _, total, summed = combine(in_ref, 4, (own,))
    attn = (summed / total).astype(BF16)
    for i in range(8):
        out_ref[i, 0:O, :] = attn
        out_ref[i, O:LAST, :] = in_ref[FAR.index(0), O + 16 : MSG, :]


def project_kernel(mine_ref, sib_ref, w_ref, out_ref):
    zh, zl, yh, core = position()
    def four(ref, which):
        a = jnp.concatenate([ref[SLOT[j], 0:O, :] for j in range(8)], axis=0)
        return dot_tn(a, w_ref[pl.ds(pl.multiple_of(which * 4 * HD, 4 * HD), 4 * HD), :])

    out = four(mine_ref, core) + four(sib_ref, 1 - core)
    for i in range(8):
        out_ref[i, :, :] = out.astype(BF16)


def block_kernel(len_ref, q_ref, k_ref, v_ref, mine_ref, sib_ref, out_ref, anchor):
    zh, zl, yh, core = position()
    ctx = ((zh * 4 + zl) * 2 + yh) * 2 + core
    for j in range(8):
        anchor[core, 16 * j : 16 * j + 16, :] = mine_ref[SLOT[j], O:LAST, :]
        anchor[1 - core, 16 * j : 16 * j + 16, :] = sib_ref[SLOT[j], O:LAST, :]
    keys = jnp.concatenate([anchor[0], k_ref[...]], axis=0)
    values = jnp.concatenate([anchor[1], v_ref[...]], axis=0)
    length = len_ref[ctx]
    first = jnp.where(ctx > 0, len_ref[0], 0)
    slot, row = rows_of((BLK, 2 * BLK), 1), rows_of((BLK, 2 * BLK), 0)
    mask = (slot < jnp.minimum(first, BLK)) | (
        (slot >= BLK) & (slot - BLK <= row) & (slot - BLK < length)
    )
    for h in range(HEADS):
        s = dot_nt(q_ref[:, h * HD : (h + 1) * HD], keys) * SCALE
        s = jnp.where(mask, s, NEG)
        e = jnp.where(mask, jnp.exp(s - jnp.max(s, axis=1, keepdims=True)), 0.0)
        total = jnp.sum(e, axis=1, keepdims=True)
        o = jnp.dot(e.astype(BF16), values, preferred_element_type=F32)
        out_ref[:, h * HD : (h + 1) * HD] = (o / total).astype(BF16)


SMEM = pl.BlockSpec(memory_space=pltpu.SMEM)
VMEM = pl.BlockSpec(memory_space=pltpu.VMEM)


def call(kernel, outs, *args, lengths=False, scratch=(), flops=0, space=VMEM):
    specs = ([SMEM] if lengths else []) + [space] * (len(args) - (1 if lengths else 0))
    moved = sum(a.size * a.dtype.itemsize for a in args)
    outs = [jax.ShapeDtypeStruct(shape, dtype) for shape, dtype in outs]
    result = pl.pallas_call(
        kernel,
        out_shape=outs,
        in_specs=specs,
        out_specs=[VMEM] * len(outs),
        scratch_shapes=scratch,
        compiler_params=pltpu.CompilerParams(vmem_limit_bytes=6 << 20),
        cost_estimate=pl.CostEstimate(flops=flops, bytes_accessed=moved, transcendentals=0),
    )(*args)
    return result if len(outs) > 1 else result[0]


def exchange(x, axes, order=None):
    groups = None if order is None else [list(order)]
    return lax.all_to_all(x, axes, 0, 0, axis_index_groups=groups, tiled=True)


SWAP = [(0, 1), (1, 0)]


def per_device(bq, bk, bv, lengths, rq, rk, rv, w):
    kv, q4 = call(
        load_kernel, [((2 * BLK, HD), BF16), ((512, HD), BF16)],
        *(pltpu.with_memory_space_constraint(a, pltpu.HBM) for a in (bk, bv, rq)),
        scratch=[pltpu.SemaphoreType.DMA((6,))], space=pl.BlockSpec(memory_space=pltpu.HBM),
    )
    sib = lax.ppermute(kv, "core", SWAP)
    own, o, st = call(
        early_kernel,
        [((O + 8, 128), F32), ((HD, 512), F32), ((8, 512), F32)],
        lengths, q4, kv, rk, rv, lengths=True, scratch=[pltpu.VMEM((HD, 128), F32)],
    )
    parts = call(
        partial_kernel, [((8, MSG, 128), BF16)], lengths, q4, kv, sib, own, o, st, lengths=True
    )
    parts = exchange(parts, GROUP, NEAR)
    grouped = call(group_kernel, [((4, MSG, 128), BF16)], parts)
    grouped = exchange(grouped, "zh", FAR)
    attn = call(final_kernel, [((8, LAST, 128), BF16)], grouped, own)
    attn = exchange(attn, GROUP, NEAR)
    attn_sib = lax.ppermute(attn, "core", SWAP)
    partial = call(project_kernel, [((8, 128, 128), BF16)], attn, attn_sib, w)
    partial = exchange(partial, "tp")
    row_output = jnp.sum(partial.astype(F32), axis=0)
    block_attention = call(
        block_kernel, [(bq.shape, BF16)], lengths, bq, bk, bv, attn, attn_sib,
        lengths=True, scratch=[pltpu.VMEM((2, BLK, HD), BF16)],
    )
    return block_attention, row_output


def solution(mesh):
    fine = Mesh(mesh.devices.reshape(4, 4, 2, 2, 8), CTX + ("tp",))
    return jax.shard_map(
        per_device,
        mesh=fine,
        in_specs=(
            P(CTX, "tp"),
            P(CTX, "tp"),
            P(CTX, "tp"),
            P(),
            P(None, "tp"),
            P(None, "tp"),
            P(None, "tp"),
            P("tp", CTX),
        ),
        out_specs=(P(CTX, "tp"), P(None, CTX)),
        check_vma=False,
    )
```

```python
import jax
import jax.numpy as jnp
from jax import lax
from jax.experimental import pallas as pl
from jax.experimental.pallas import tpu as pltpu
from jax.sharding import Mesh, PartitionSpec as P

HD = 128
BLK = 128
HEADS = 8
SCALE = HD ** (-0.5)
NEG = -1e30
CTX = ("zh", "zl", "yh", "core")
FAR = (2, 0, 3, 1)
NEAR = (5, 4, 7, 6, 1, 0, 3, 2)
BACK = (7, 6, 5, 4, 3, 2, 1, 0)
TP = (5, 4, 7, 6, 1, 0, 3, 2)
SLOT = tuple(NEAR.index(j) for j in range(8))
RSLOT = tuple(BACK.index(j) for j in range(8))
GROUP = ("zl", "yh")
O = 64
MSG = 88
LAST = 80
F32, BF16 = jnp.float32, jnp.bfloat16


def dot_nt(a, b):
    return lax.dot_general(a, b, (((1,), (1,)), ((), ())), preferred_element_type=F32)


def dot_tn(a, b):
    return lax.dot_general(a, b, (((0,), (0,)), ((), ())), preferred_element_type=F32)


def rows_of(shape, dim):
    return lax.broadcasted_iota(jnp.int32, shape, dim)


def split(x):
    high = x.astype(BF16).astype(F32)
    return high, (x - high).astype(BF16).astype(F32)


def position():
    zh, zl, yh, core = (lax.axis_index(a) for a in CTX)
    return zh, zl, yh, core


def statistics(m_high, m_low, total):
    t_high, t_low = split(total)
    r = rows_of((8, total.shape[1]), 0)
    zero = jnp.zeros(r.shape, F32)
    out = jnp.where(r == 0, m_high, zero)
    out = jnp.where(r == 1, m_low, out)
    out = jnp.where(r == 2, t_high, out)
    return jnp.where(r == 3, t_low, out)


def column_softmax(scores, mask):
    scores = jnp.where(mask, scores, NEG)
    high, low = split(jnp.max(scores, axis=0, keepdims=True))
    e = jnp.where(mask, jnp.exp(scores - (high + low)), 0.0)
    return high, low, e


def heads_softmax(scores, mask):
    high, low, e = column_softmax(scores, mask)
    return high, low, jnp.sum(e, axis=0, keepdims=True), e.astype(BF16)


def load_kernel(k_ref, v_ref, q_ref, kv_ref, q4_ref, sem):
    core = lax.axis_index("core")
    copies = [
        pltpu.make_async_copy(k_ref, kv_ref.at[0:BLK], sem.at[0]),
        pltpu.make_async_copy(v_ref, kv_ref.at[BLK : 2 * BLK], sem.at[1]),
    ]
    for i in range(4):
        columns = pl.ds(pl.multiple_of((core * 4 + i) * HD, HD), HD)
        rows = slice(i * BLK, (i + 1) * BLK)
        copies.append(pltpu.make_async_copy(q_ref.at[:, columns], q4_ref.at[rows], sem.at[2 + i]))
    for c in copies:
        c.start()
    for c in copies:
        c.wait()


def early_kernel(len_ref, q_ref, kv_ref, rk_ref, rv_ref, own_ref, o_ref, st_ref, scratch):
    zh, zl, yh, core = position()
    ctx = ((zh * 4 + zl) * 2 + yh) * 2 + core
    s = dot_nt(kv_ref[0:BLK, :], q_ref[...]) * SCALE
    own = dot_nt(rk_ref[...], q_ref[pl.ds(pl.multiple_of(zl * HD, HD), HD), :]) * SCALE
    high, low, total, e = heads_softmax(s, rows_of(s.shape, 0) < len_ref[ctx])
    o_ref[...] = dot_tn(kv_ref[BLK:, :], e)
    r = rows_of((8, 512), 0)
    st_ref[...] = jnp.where(r == 0, high, jnp.where(r == 1, low, total))
    high, low, total, e = heads_softmax(own, rows_of(own.shape, 0) <= rows_of(own.shape, 1))
    scratch[...] = dot_tn(rv_ref[...], e)
    own_ref[0:O, :] = scratch[pl.ds(pl.multiple_of(yh * O, O), O), :]
    r = rows_of((8, 128), 0)
    own_ref[O : O + 8, :] = jnp.where(r == 0, high + low, total)


def partial_kernel(len_ref, q_ref, kv_ref, sib_ref, own_ref, o_ref, st_ref, out_ref):
    zh, zl, yh, core = position()
    ctx = ((zh * 4 + zl) * 2 + yh) * 2 + core
    s = dot_nt(sib_ref[0:BLK, :], q_ref[...]) * SCALE
    high, low, total, e = heads_softmax(s, rows_of(s.shape, 0) < len_ref[ctx + 1 - 2 * core])
    o = dot_tn(sib_ref[BLK:, :], e)
    high_a, low_a, total_a = st_ref[0:1, :], st_ref[1:2, :], st_ref[2:3, :]
    better = high_a + low_a > high + low
    top_high, top_low = jnp.where(better, high_a, high), jnp.where(better, low_a, low)
    top = top_high + top_low
    wa, wb = jnp.exp(high_a + low_a - top), jnp.exp(high + low - top)
    stats = statistics(top_high, top_low, total_a * wa + total * wb)
    o = o_ref[...] * wa + o * wb
    first = jnp.where(core == 0, kv_ref[0:BLK, :].astype(F32), sib_ref[BLK:, :].astype(F32))
    for j in range(8):
        cols = slice(j // 2 * HD, (j // 2 + 1) * HD)
        rows = [o[j % 2 * O : (j % 2 + 1) * O, cols], stats[:, cols], first[16 * j : 16 * j + 16]]
        out_ref[SLOT[j]] = jnp.concatenate(rows, axis=0).astype(BF16)


def combine(ref, count, more=()):
    ms, ts, os = [], [], []
    for i in range(count):
        message = ref[i].astype(F32)
        st = message[O : O + 8]
        ms.append((st[0:1], st[1:2]))
        ts.append(st[2:3] + st[3:4])
        os.append(message[0:O])
    high, low = ms[0]
    for h, l in ms[1:]:
        better = h + l > high + low
        high, low = jnp.where(better, h, high), jnp.where(better, l, low)
    top = high + low
    for m, _, _ in more:
        top = jnp.maximum(top, m)
    total = jnp.zeros_like(top)
    summed = jnp.zeros((O, 128), F32)
    for (h, l), t, o in zip(ms, ts, os):
        w = jnp.exp(h + l - top)
        total, summed = total + t * w, summed + o * w
    for m, t, o in more:
        w = jnp.exp(m - top)
        total, summed = total + t * w, summed + o * w
    return high, low, total, summed


def group_kernel(in_ref, out_ref):
    high, low, total, summed = combine(in_ref, 8)
    first = in_ref[SLOT[0]].astype(F32)[O + 8 : MSG]
    message = jnp.concatenate([summed, statistics(high, low, total), first], axis=0).astype(BF16)
    for i in range(4):
        out_ref[i] = message


def final_kernel(in_ref, own_ref, out_ref):
    own = (own_ref[O : O + 1, :], own_ref[O + 1 : O + 2, :], own_ref[0:O, :])
    _, _, total, summed = combine(in_ref, 4, (own,))
    first = in_ref[FAR.index(0)].astype(F32)[O + 8 : MSG]
    message = jnp.concatenate([summed / total, first], axis=0).astype(BF16)
    for i in range(8):
        out_ref[i] = message


def project_kernel(mine_ref, sib_ref, w_ref, out_ref):
    zh, zl, yh, core = position()
    def four(ref, which):
        a = jnp.concatenate([ref[RSLOT[j], 0:O, :] for j in range(8)], axis=0)
        return dot_tn(a, w_ref[pl.ds(pl.multiple_of(which * 4 * HD, 4 * HD), 4 * HD), :])

    out = four(mine_ref, core) + four(sib_ref, 1 - core)
    for i in range(8):
        out_ref[i, :, :] = out.astype(BF16)


def block_kernel(len_ref, q_ref, k_ref, v_ref, mine_ref, sib_ref, out_ref, anchor):
    zh, zl, yh, core = position()
    ctx = ((zh * 4 + zl) * 2 + yh) * 2 + core
    for j in range(8):
        anchor[core, 16 * j : 16 * j + 16, :] = mine_ref[RSLOT[j], O:LAST, :]
        anchor[1 - core, 16 * j : 16 * j + 16, :] = sib_ref[RSLOT[j], O:LAST, :]
    keys = jnp.concatenate([anchor[0], k_ref[...]], axis=0)
    values = jnp.concatenate([anchor[1], v_ref[...]], axis=0)
    length = len_ref[ctx]
    first = jnp.where(ctx > 0, len_ref[0], 0)
    slot, row = rows_of((BLK, 2 * BLK), 1), rows_of((BLK, 2 * BLK), 0)
    mask = (slot < jnp.minimum(first, BLK)) | (
        (slot >= BLK) & (slot - BLK <= row) & (slot - BLK < length)
    )
    for h in range(HEADS):
        s = dot_nt(q_ref[:, h * HD : (h + 1) * HD], keys) * SCALE
        s = jnp.where(mask, s, NEG)
        e = jnp.where(mask, jnp.exp(s - jnp.max(s, axis=1, keepdims=True)), 0.0)
        total = jnp.sum(e, axis=1, keepdims=True)
        o = jnp.dot(e.astype(BF16), values, preferred_element_type=F32)
        out_ref[:, h * HD : (h + 1) * HD] = (o / total).astype(BF16)


SMEM = pl.BlockSpec(memory_space=pltpu.SMEM)
VMEM = pl.BlockSpec(memory_space=pltpu.VMEM)


def call(kernel, outs, *args, lengths=False, scratch=(), flops=0, space=VMEM):
    specs = ([SMEM] if lengths else []) + [space] * (len(args) - (1 if lengths else 0))
    moved = sum(a.size * a.dtype.itemsize for a in args)
    outs = [jax.ShapeDtypeStruct(shape, dtype) for shape, dtype in outs]
    result = pl.pallas_call(
        kernel,
        out_shape=outs,
        in_specs=specs,
        out_specs=[VMEM] * len(outs),
        scratch_shapes=scratch,
        compiler_params=pltpu.CompilerParams(vmem_limit_bytes=6 << 20),
        cost_estimate=pl.CostEstimate(flops=flops, bytes_accessed=moved, transcendentals=0),
    )(*args)
    return result if len(outs) > 1 else result[0]


def exchange(x, axes, order=None):
    groups = None if order is None else [list(order)]
    return lax.all_to_all(x, axes, 0, 0, axis_index_groups=groups, tiled=True)


SWAP = [(0, 1), (1, 0)]


def per_device(bq, bk, bv, lengths, rq, rk, rv, w):
    kv, q4 = call(
        load_kernel, [((2 * BLK, HD), BF16), ((512, HD), BF16)],
        *(pltpu.with_memory_space_constraint(a, pltpu.HBM) for a in (bk, bv, rq)),
        scratch=[pltpu.SemaphoreType.DMA((6,))], space=pl.BlockSpec(memory_space=pltpu.HBM),
    )
    sib = lax.ppermute(kv, "core", SWAP)
    own, o, st = call(
        early_kernel,
        [((O + 8, 128), F32), ((HD, 512), F32), ((8, 512), F32)],
        lengths, q4, kv, rk, rv, lengths=True, scratch=[pltpu.VMEM((HD, 128), F32)],
    )
    parts = call(
        partial_kernel, [((8, MSG, 128), BF16)], lengths, q4, kv, sib, own, o, st, lengths=True
    )
    parts = exchange(parts, GROUP, NEAR)
    grouped = call(group_kernel, [((4, MSG, 128), BF16)], parts)
    grouped = exchange(grouped, "zh", FAR)
    attn = call(final_kernel, [((8, LAST, 128), BF16)], grouped, own)
    attn = exchange(attn, GROUP, BACK)
    attn_sib = lax.ppermute(attn, "core", SWAP)
    partial = call(project_kernel, [((8, 128, 128), BF16)], attn, attn_sib, w)
    partial = exchange(partial, "tp", TP)
    row_output = jnp.sum(partial.astype(F32), axis=0)
    block_attention = call(
        block_kernel, [(bq.shape, BF16)], lengths, bq, bk, bv, attn, attn_sib,
        lengths=True, scratch=[pltpu.VMEM((2, BLK, HD), BF16)],
    )
    return block_attention, row_output


def solution(mesh):
    fine = Mesh(mesh.devices.reshape(4, 4, 2, 2, 8), CTX + ("tp",))
    return jax.shard_map(
        per_device,
        mesh=fine,
        in_specs=(
            P(CTX, "tp"),
            P(CTX, "tp"),
            P(CTX, "tp"),
            P(),
            P(None, "tp"),
            P(None, "tp"),
            P(None, "tp"),
            P("tp", CTX),
        ),
        out_specs=(P(CTX, "tp"), P(None, CTX)),
        check_vma=False,
    )
```

```python
import jax
import jax.numpy as jnp
from jax import lax
from jax.experimental import pallas as pl
from jax.experimental.pallas import tpu as pltpu
from jax.sharding import Mesh, PartitionSpec as P

HD = 128
BLK = 128
HEADS = 8
SCALE = HD ** (-0.5)
NEG = -1e30
CTX = ("zh", "zl", "yh", "core")
FAR = (2, 3, 0, 1)
NEAR = (5, 0, 2, 6, 1, 4, 3, 7)
BACK = (5, 4, 7, 6, 1, 0, 3, 2)
TP = (5, 4, 7, 6, 1, 0, 3, 2)
SLOT = tuple(NEAR.index(j) for j in range(8))
RSLOT = tuple(BACK.index(j) for j in range(8))
GROUP = ("zl", "yh")
O = 64
MSG = 88
LAST = 80
F32, BF16 = jnp.float32, jnp.bfloat16


def dot_nt(a, b):
    return lax.dot_general(a, b, (((1,), (1,)), ((), ())), preferred_element_type=F32)


def dot_tn(a, b):
    return lax.dot_general(a, b, (((0,), (0,)), ((), ())), preferred_element_type=F32)


def rows_of(shape, dim):
    return lax.broadcasted_iota(jnp.int32, shape, dim)


def split(x):
    high = x.astype(BF16).astype(F32)
    return high, (x - high).astype(BF16).astype(F32)


def position():
    zh, zl, yh, core = (lax.axis_index(a) for a in CTX)
    return zh, zl, yh, core


def heads_class(zh, core):
    return jnp.where(zh == 0, 1 - core, core)


def statistics(m_high, m_low, total):
    t_high, t_low = split(total)
    r = rows_of((8, total.shape[1]), 0)
    zero = jnp.zeros(r.shape, F32)
    out = jnp.where(r == 0, m_high, zero)
    out = jnp.where(r == 1, m_low, out)
    out = jnp.where(r == 2, t_high, out)
    return jnp.where(r == 3, t_low, out)


def column_softmax(scores, mask):
    scores = jnp.where(mask, scores, NEG)
    high, low = split(jnp.max(scores, axis=0, keepdims=True))
    e = jnp.where(mask, jnp.exp(scores - (high + low)), 0.0)
    return high, low, e


def heads_softmax(scores, mask):
    high, low, e = column_softmax(scores, mask)
    return high, low, jnp.sum(e, axis=0, keepdims=True), e.astype(BF16)


def load_kernel(k_ref, v_ref, q_ref, kv_ref, q4_ref, sem):
    zh, zl, yh, core = position()
    first = heads_class(zh, core) * 4
    copies = [
        pltpu.make_async_copy(k_ref, kv_ref.at[0:BLK], sem.at[0]),
        pltpu.make_async_copy(v_ref, kv_ref.at[BLK : 2 * BLK], sem.at[1]),
    ]
    for i in range(4):
        columns = pl.ds(pl.multiple_of((first + i) * HD, HD), HD)
        rows = slice(i * BLK, (i + 1) * BLK)
        copies.append(pltpu.make_async_copy(q_ref.at[:, columns], q4_ref.at[rows], sem.at[2 + i]))
    for c in copies:
        c.start()
    for c in copies:
        c.wait()


def early_kernel(len_ref, q_ref, kv_ref, rk_ref, rv_ref, own_ref, o_ref, st_ref, scratch):
    zh, zl, yh, core = position()
    ctx = ((zh * 4 + zl) * 2 + yh) * 2 + core
    s = dot_nt(kv_ref[0:BLK, :], q_ref[...]) * SCALE
    own = dot_nt(rk_ref[...], q_ref[pl.ds(pl.multiple_of(zl * HD, HD), HD), :]) * SCALE
    high, low, total, e = heads_softmax(s, rows_of(s.shape, 0) < len_ref[ctx])
    o_ref[...] = dot_tn(kv_ref[BLK:, :], e)
    r = rows_of((8, 512), 0)
    st_ref[...] = jnp.where(r == 0, high, jnp.where(r == 1, low, total))
    high, low, total, e = heads_softmax(own, rows_of(own.shape, 0) <= rows_of(own.shape, 1))
    scratch[...] = dot_tn(rv_ref[...], e)
    own_ref[0:O, :] = scratch[pl.ds(pl.multiple_of(yh * O, O), O), :]
    r = rows_of((8, 128), 0)
    own_ref[O : O + 8, :] = jnp.where(r == 0, high + low, total)


def partial_kernel(len_ref, q_ref, kv_ref, sib_ref, own_ref, o_ref, st_ref, out_ref):
    zh, zl, yh, core = position()
    ctx = ((zh * 4 + zl) * 2 + yh) * 2 + core
    s = dot_nt(sib_ref[0:BLK, :], q_ref[...]) * SCALE
    high, low, total, e = heads_softmax(s, rows_of(s.shape, 0) < len_ref[ctx + 1 - 2 * core])
    o = dot_tn(sib_ref[BLK:, :], e)
    high_a, low_a, total_a = st_ref[0:1, :], st_ref[1:2, :], st_ref[2:3, :]
    better = high_a + low_a > high + low
    top_high, top_low = jnp.where(better, high_a, high), jnp.where(better, low_a, low)
    top = top_high + top_low
    wa, wb = jnp.exp(high_a + low_a - top), jnp.exp(high + low - top)
    stats = statistics(top_high, top_low, total_a * wa + total * wb)
    o = o_ref[...] * wa + o * wb
    cls = heads_class(zh, core)
    first = jnp.where(cls == 0, sib_ref[0:BLK, :].astype(F32), kv_ref[BLK:, :].astype(F32))
    for j in range(8):
        cols = slice(j // 2 * HD, (j // 2 + 1) * HD)
        rows = [o[j % 2 * O : (j % 2 + 1) * O, cols], stats[:, cols], first[16 * j : 16 * j + 16]]
        out_ref[SLOT[j]] = jnp.concatenate(rows, axis=0).astype(BF16)


def combine(ref, count, more=()):
    ms, ts, os = [], [], []
    for i in range(count):
        message = ref[i].astype(F32)
        st = message[O : O + 8]
        ms.append((st[0:1], st[1:2]))
        ts.append(st[2:3] + st[3:4])
        os.append(message[0:O])
    high, low = ms[0]
    for h, l in ms[1:]:
        better = h + l > high + low
        high, low = jnp.where(better, h, high), jnp.where(better, l, low)
    top = high + low
    for m, _, _ in more:
        top = jnp.maximum(top, m)
    total = jnp.zeros_like(top)
    summed = jnp.zeros((O, 128), F32)
    for (h, l), t, o in zip(ms, ts, os):
        w = jnp.exp(h + l - top)
        total, summed = total + t * w, summed + o * w
    for m, t, o in more:
        w = jnp.exp(m - top)
        total, summed = total + t * w, summed + o * w
    return high, low, total, summed


def group_kernel(in_ref, out_ref):
    high, low, total, summed = combine(in_ref, 8)
    first = in_ref[SLOT[0]].astype(F32)[O + 8 : MSG]
    message = jnp.concatenate([summed, statistics(high, low, total), first], axis=0).astype(BF16)
    for i in range(4):
        out_ref[i] = message


def final_kernel(in_ref, own_ref, out_ref):
    own = (own_ref[O : O + 1, :], own_ref[O + 1 : O + 2, :], own_ref[0:O, :])
    _, _, total, summed = combine(in_ref, 4, (own,))
    first = in_ref[FAR.index(0)].astype(F32)[O + 8 : MSG]
    message = jnp.concatenate([summed / total, first], axis=0).astype(BF16)
    for i in range(8):
        out_ref[i] = message


def project_kernel(mine_ref, sib_ref, w_ref, out_ref):
    zh, zl, yh, core = position()
    def four(ref, which):
        a = jnp.concatenate([ref[RSLOT[j], 0:O, :] for j in range(8)], axis=0)
        return dot_tn(a, w_ref[pl.ds(pl.multiple_of(which * 4 * HD, 4 * HD), 4 * HD), :])

    cls = heads_class(zh, core)
    out = four(mine_ref, cls) + four(sib_ref, 1 - cls)
    for i in range(8):
        out_ref[i, :, :] = out.astype(BF16)


def block_kernel(len_ref, q_ref, k_ref, v_ref, mine_ref, sib_ref, out_ref, anchor):
    zh, zl, yh, core = position()
    ctx = ((zh * 4 + zl) * 2 + yh) * 2 + core
    cls = heads_class(zh, core)
    for j in range(8):
        anchor[cls, 16 * j : 16 * j + 16, :] = mine_ref[RSLOT[j], O:LAST, :]
        anchor[1 - cls, 16 * j : 16 * j + 16, :] = sib_ref[RSLOT[j], O:LAST, :]
    keys = jnp.concatenate([anchor[0], k_ref[...]], axis=0)
    values = jnp.concatenate([anchor[1], v_ref[...]], axis=0)
    length = len_ref[ctx]
    first = jnp.where(ctx > 0, len_ref[0], 0)
    slot, row = rows_of((BLK, 2 * BLK), 1), rows_of((BLK, 2 * BLK), 0)
    mask = (slot < jnp.minimum(first, BLK)) | (
        (slot >= BLK) & (slot - BLK <= row) & (slot - BLK < length)
    )
    for h in range(HEADS):
        s = dot_nt(q_ref[:, h * HD : (h + 1) * HD], keys) * SCALE
        s = jnp.where(mask, s, NEG)
        e = jnp.where(mask, jnp.exp(s - jnp.max(s, axis=1, keepdims=True)), 0.0)
        total = jnp.sum(e, axis=1, keepdims=True)
        o = jnp.dot(e.astype(BF16), values, preferred_element_type=F32)
        out_ref[:, h * HD : (h + 1) * HD] = (o / total).astype(BF16)


SMEM = pl.BlockSpec(memory_space=pltpu.SMEM)
VMEM = pl.BlockSpec(memory_space=pltpu.VMEM)


def call(kernel, outs, *args, lengths=False, scratch=(), flops=0, space=VMEM):
    specs = ([SMEM] if lengths else []) + [space] * (len(args) - (1 if lengths else 0))
    moved = sum(a.size * a.dtype.itemsize for a in args)
    outs = [jax.ShapeDtypeStruct(shape, dtype) for shape, dtype in outs]
    result = pl.pallas_call(
        kernel,
        out_shape=outs,
        in_specs=specs,
        out_specs=[VMEM] * len(outs),
        scratch_shapes=scratch,
        compiler_params=pltpu.CompilerParams(vmem_limit_bytes=6 << 20),
        cost_estimate=pl.CostEstimate(flops=flops, bytes_accessed=moved, transcendentals=0),
    )(*args)
    return result if len(outs) > 1 else result[0]


def exchange(x, axes, *orders):
    groups = [list(order) for order in orders]
    return lax.all_to_all(x, axes, 0, 0, axis_index_groups=groups, tiled=True)


def carriers(cls):
    return [zh * 2 + (1 - cls if zh == 0 else cls) for zh in FAR]


SWAP = [(0, 1), (1, 0)]


def per_device(bq, bk, bv, lengths, rq, rk, rv, w):
    kv, q4 = call(
        load_kernel, [((2 * BLK, HD), BF16), ((512, HD), BF16)],
        *(pltpu.with_memory_space_constraint(a, pltpu.HBM) for a in (bk, bv, rq)),
        scratch=[pltpu.SemaphoreType.DMA((6,))], space=pl.BlockSpec(memory_space=pltpu.HBM),
    )
    sib = lax.ppermute(kv, "core", SWAP)
    own, o, st = call(
        early_kernel,
        [((O + 8, 128), F32), ((HD, 512), F32), ((8, 512), F32)],
        lengths, q4, kv, rk, rv, lengths=True, scratch=[pltpu.VMEM((HD, 128), F32)],
    )
    parts = call(
        partial_kernel, [((8, MSG, 128), BF16)], lengths, q4, kv, sib, own, o, st, lengths=True
    )
    parts = exchange(parts, GROUP, NEAR)
    grouped = call(group_kernel, [((4, MSG, 128), BF16)], parts)
    grouped = exchange(grouped, ("zh", "core"), carriers(0), carriers(1))
    attn = call(final_kernel, [((8, LAST, 128), BF16)], grouped, own)
    attn = exchange(attn, GROUP, BACK)
    attn_sib = lax.ppermute(attn, "core", SWAP)
    partial = call(project_kernel, [((8, 128, 128), BF16)], attn, attn_sib, w)
    partial = exchange(partial, "tp", TP)
    row_output = jnp.sum(partial.astype(F32), axis=0)
    block_attention = call(
        block_kernel, [(bq.shape, BF16)], lengths, bq, bk, bv, attn, attn_sib,
        lengths=True, scratch=[pltpu.VMEM((2, BLK, HD), BF16)],
    )
    return block_attention, row_output


def solution(mesh):
    fine = Mesh(mesh.devices.reshape(4, 4, 2, 2, 8), CTX + ("tp",))
    return jax.shard_map(
        per_device,
        mesh=fine,
        in_specs=(
            P(CTX, "tp"),
            P(CTX, "tp"),
            P(CTX, "tp"),
            P(),
            P(None, "tp"),
            P(None, "tp"),
            P(None, "tp"),
            P("tp", CTX),
        ),
        out_specs=(P(CTX, "tp"), P(None, CTX)),
        check_vma=False,
    )
```

```python
import jax
import jax.numpy as jnp
from jax import lax
from jax.experimental import pallas as pl
from jax.experimental.pallas import tpu as pltpu
from jax.sharding import Mesh, PartitionSpec as P

HD = 128
BLK = 128
HEADS = 8
SCALE = HD ** (-0.5)
NEG = -1e30
CTX = ("zh", "zl", "yh", "core")
FAR = (2, 3, 0, 1)
NEAR = (5, 0, 2, 6, 1, 4, 3, 7)
BACK = (5, 4, 7, 6, 1, 0, 3, 2)
TP = (5, 4, 7, 6, 1, 0, 3, 2)
SLOT = tuple(NEAR.index(j) for j in range(8))
RSLOT = tuple(BACK.index(j) for j in range(8))
GROUP = ("zl", "yh")
O = 64
MSG = 88
LAST = 80
F32, BF16 = jnp.float32, jnp.bfloat16


def dot_nt(a, b):
    return lax.dot_general(a, b, (((1,), (1,)), ((), ())), preferred_element_type=F32)


def dot_tn(a, b):
    return lax.dot_general(a, b, (((0,), (0,)), ((), ())), preferred_element_type=F32)


def rows_of(shape, dim):
    return lax.broadcasted_iota(jnp.int32, shape, dim)


def split(x):
    high = x.astype(BF16).astype(F32)
    return high, (x - high).astype(BF16).astype(F32)


def position():
    zh, zl, yh, core = (lax.axis_index(a) for a in CTX)
    return zh, zl, yh, core


def heads_class(zh, core):
    return jnp.where(zh == 0, 1 - core, core)


def statistics(m_high, m_low, total):
    t_high, t_low = split(total)
    r = rows_of((8, total.shape[1]), 0)
    zero = jnp.zeros(r.shape, F32)
    out = jnp.where(r == 0, m_high, zero)
    out = jnp.where(r == 1, m_low, out)
    out = jnp.where(r == 2, t_high, out)
    return jnp.where(r == 3, t_low, out)


def column_softmax(scores, mask):
    scores = jnp.where(mask, scores, NEG)
    high, low = split(jnp.max(scores, axis=0, keepdims=True))
    e = jnp.where(mask, jnp.exp(scores - (high + low)), 0.0)
    return high, low, e


def heads_softmax(scores, mask):
    high, low, e = column_softmax(scores, mask)
    return high, low, jnp.sum(e, axis=0, keepdims=True), e.astype(BF16)


def load_kernel(k_ref, v_ref, q_ref, kv_ref, q4_ref, sem):
    zh, zl, yh, core = position()
    first = heads_class(zh, core) * 4
    copies = [
        pltpu.make_async_copy(k_ref, kv_ref.at[0:BLK], sem.at[0]),
        pltpu.make_async_copy(v_ref, kv_ref.at[BLK : 2 * BLK], sem.at[1]),
    ]
    for i in range(4):
        columns = pl.ds(pl.multiple_of((first + i) * HD, HD), HD)
        rows = slice(i * BLK, (i + 1) * BLK)
        copies.append(pltpu.make_async_copy(q_ref.at[:, columns], q4_ref.at[rows], sem.at[2 + i]))
    for c in copies:
        c.start()
    for c in copies:
        c.wait()


def early_kernel(len_ref, q_ref, kv_ref, rk_ref, rv_ref, own_ref, o_ref, st_ref, scratch):
    zh, zl, yh, core = position()
    ctx = ((zh * 4 + zl) * 2 + yh) * 2 + core
    s = dot_nt(kv_ref[0:BLK, :], q_ref[...]) * SCALE
    own = dot_nt(rk_ref[...], q_ref[pl.ds(pl.multiple_of(zl * HD, HD), HD), :]) * SCALE
    high, low, total, e = heads_softmax(s, rows_of(s.shape, 0) < len_ref[ctx])
    o_ref[...] = dot_tn(kv_ref[BLK:, :], e)
    r = rows_of((8, 512), 0)
    st_ref[...] = jnp.where(r == 0, high, jnp.where(r == 1, low, total))
    high, low, total, e = heads_softmax(own, rows_of(own.shape, 0) <= rows_of(own.shape, 1))
    scratch[...] = dot_tn(rv_ref[...], e)
    own_ref[0:O, :] = scratch[pl.ds(pl.multiple_of(yh * O, O), O), :]
    r = rows_of((8, 128), 0)
    own_ref[O : O + 8, :] = jnp.where(r == 0, high + low, total)


def partial_kernel(len_ref, q_ref, kv_ref, sib_ref, own_ref, o_ref, st_ref, out_ref):
    zh, zl, yh, core = position()
    ctx = ((zh * 4 + zl) * 2 + yh) * 2 + core
    s = dot_nt(sib_ref[0:BLK, :], q_ref[...]) * SCALE
    high, low, total, e = heads_softmax(s, rows_of(s.shape, 0) < len_ref[ctx + 1 - 2 * core])
    o = dot_tn(sib_ref[BLK:, :], e)
    high_a, low_a, total_a = st_ref[0:1, :], st_ref[1:2, :], st_ref[2:3, :]
    better = high_a + low_a > high + low
    top_high, top_low = jnp.where(better, high_a, high), jnp.where(better, low_a, low)
    top = top_high + top_low
    wa, wb = jnp.exp(high_a + low_a - top), jnp.exp(high + low - top)
    stats = statistics(top_high, top_low, total_a * wa + total * wb)
    o = o_ref[...] * wa + o * wb
    cls = heads_class(zh, core)
    first = jnp.where(cls == 0, sib_ref[0:BLK, :].astype(F32), kv_ref[BLK:, :].astype(F32))
    for j in range(8):
        cols = slice(j // 2 * HD, (j // 2 + 1) * HD)
        rows = [o[j % 2 * O : (j % 2 + 1) * O, cols], stats[:, cols], first[16 * j : 16 * j + 16]]
        out_ref[SLOT[j]] = jnp.concatenate(rows, axis=0).astype(BF16)


def combine(ref, count, more=()):
    ms, ts, os = [], [], []
    for i in range(count):
        message = ref[i].astype(F32)
        st = message[O : O + 8]
        ms.append((st[0:1], st[1:2]))
        ts.append(st[2:3] + st[3:4])
        os.append(message[0:O])
    high, low = ms[0]
    for h, l in ms[1:]:
        better = h + l > high + low
        high, low = jnp.where(better, h, high), jnp.where(better, l, low)
    top = high + low
    for m, _, _ in more:
        top = jnp.maximum(top, m)
    total = jnp.zeros_like(top)
    summed = jnp.zeros((O, 128), F32)
    for (h, l), t, o in zip(ms, ts, os):
        w = jnp.exp(h + l - top)
        total, summed = total + t * w, summed + o * w
    for m, t, o in more:
        w = jnp.exp(m - top)
        total, summed = total + t * w, summed + o * w
    return high, low, total, summed


def group_kernel(in_ref, out_ref):
    high, low, total, summed = combine(in_ref, 8)
    first = in_ref[SLOT[0]].astype(F32)[O + 8 : MSG]
    message = jnp.concatenate([summed, statistics(high, low, total), first], axis=0).astype(BF16)
    for i in range(4):
        out_ref[i] = message


def final_kernel(in_ref, own_ref, out_ref):
    own = (own_ref[O : O + 1, :], own_ref[O + 1 : O + 2, :], own_ref[0:O, :])
    _, _, total, summed = combine(in_ref, 4, (own,))
    first = in_ref[FAR.index(0)].astype(F32)[O + 8 : MSG]
    message = jnp.concatenate([summed / total, first], axis=0).astype(BF16)
    for i in range(8):
        out_ref[i] = message


def four(ref, w_ref, cls):
    a = jnp.concatenate([ref[RSLOT[j], 0:O, :] for j in range(8)], axis=0)
    return dot_tn(a, w_ref[pl.ds(pl.multiple_of(cls * 4 * HD, 4 * HD), 4 * HD), :])


def half_kernel(mine_ref, w_ref, out_ref):
    zh, zl, yh, core = position()
    out_ref[...] = four(mine_ref, w_ref, heads_class(zh, core))


def project_kernel(half_ref, sib_ref, w_ref, out_ref):
    zh, zl, yh, core = position()
    out = (half_ref[...] + four(sib_ref, w_ref, 1 - heads_class(zh, core))).astype(BF16)
    for i in range(8):
        out_ref[i, :, :] = out


def block_kernel(len_ref, q_ref, k_ref, v_ref, mine_ref, sib_ref, out_ref, anchor):
    zh, zl, yh, core = position()
    ctx = ((zh * 4 + zl) * 2 + yh) * 2 + core
    cls = heads_class(zh, core)
    for j in range(8):
        anchor[cls, 16 * j : 16 * j + 16, :] = mine_ref[RSLOT[j], O:LAST, :]
        anchor[1 - cls, 16 * j : 16 * j + 16, :] = sib_ref[RSLOT[j], O:LAST, :]
    keys = jnp.concatenate([anchor[0], k_ref[...]], axis=0)
    values = jnp.concatenate([anchor[1], v_ref[...]], axis=0)
    length = len_ref[ctx]
    first = jnp.where(ctx > 0, len_ref[0], 0)
    slot, row = rows_of((BLK, 2 * BLK), 1), rows_of((BLK, 2 * BLK), 0)
    mask = (slot < jnp.minimum(first, BLK)) | (
        (slot >= BLK) & (slot - BLK <= row) & (slot - BLK < length)
    )
    for h in range(HEADS):
        s = dot_nt(q_ref[:, h * HD : (h + 1) * HD], keys) * SCALE
        s = jnp.where(mask, s, NEG)
        e = jnp.where(mask, jnp.exp(s - jnp.max(s, axis=1, keepdims=True)), 0.0)
        total = jnp.sum(e, axis=1, keepdims=True)
        o = jnp.dot(e.astype(BF16), values, preferred_element_type=F32)
        out_ref[:, h * HD : (h + 1) * HD] = (o / total).astype(BF16)


SMEM = pl.BlockSpec(memory_space=pltpu.SMEM)
VMEM = pl.BlockSpec(memory_space=pltpu.VMEM)


def call(kernel, outs, *args, lengths=False, scratch=(), flops=0, space=VMEM):
    specs = ([SMEM] if lengths else []) + [space] * (len(args) - (1 if lengths else 0))
    moved = sum(a.size * a.dtype.itemsize for a in args)
    outs = [jax.ShapeDtypeStruct(shape, dtype) for shape, dtype in outs]
    result = pl.pallas_call(
        kernel,
        out_shape=outs,
        in_specs=specs,
        out_specs=[VMEM] * len(outs),
        scratch_shapes=scratch,
        compiler_params=pltpu.CompilerParams(vmem_limit_bytes=6 << 20),
        cost_estimate=pl.CostEstimate(flops=flops, bytes_accessed=moved, transcendentals=0),
    )(*args)
    return result if len(outs) > 1 else result[0]


def exchange(x, axes, *orders):
    groups = [list(order) for order in orders]
    return lax.all_to_all(x, axes, 0, 0, axis_index_groups=groups, tiled=True)


def carriers(cls):
    return [zh * 2 + (1 - cls if zh == 0 else cls) for zh in FAR]


SWAP = [(0, 1), (1, 0)]


def per_device(bq, bk, bv, lengths, rq, rk, rv, w):
    kv, q4 = call(
        load_kernel, [((2 * BLK, HD), BF16), ((512, HD), BF16)],
        *(pltpu.with_memory_space_constraint(a, pltpu.HBM) for a in (bk, bv, rq)),
        scratch=[pltpu.SemaphoreType.DMA((6,))], space=pl.BlockSpec(memory_space=pltpu.HBM),
    )
    sib = lax.ppermute(kv, "core", SWAP)
    own, o, st = call(
        early_kernel,
        [((O + 8, 128), F32), ((HD, 512), F32), ((8, 512), F32)],
        lengths, q4, kv, rk, rv, lengths=True, scratch=[pltpu.VMEM((HD, 128), F32)],
    )
    parts = call(
        partial_kernel, [((8, MSG, 128), BF16)], lengths, q4, kv, sib, own, o, st, lengths=True
    )
    parts = exchange(parts, GROUP, NEAR)
    grouped = call(group_kernel, [((4, MSG, 128), BF16)], parts)
    grouped = exchange(grouped, ("zh", "core"), carriers(0), carriers(1))
    attn = call(final_kernel, [((8, LAST, 128), BF16)], grouped, own)
    attn = exchange(attn, GROUP, BACK)
    attn_sib = lax.ppermute(attn, "core", SWAP)
    half = call(half_kernel, [((128, 128), F32)], attn, w)
    partial = call(project_kernel, [((8, 128, 128), BF16)], half, attn_sib, w)
    partial = exchange(partial, "tp", TP)
    row_output = jnp.sum(partial.astype(F32), axis=0)
    block_attention = call(
        block_kernel, [(bq.shape, BF16)], lengths, bq, bk, bv, attn, attn_sib,
        lengths=True, scratch=[pltpu.VMEM((2, BLK, HD), BF16)],
    )
    return block_attention, row_output


def solution(mesh):
    fine = Mesh(mesh.devices.reshape(4, 4, 2, 2, 8), CTX + ("tp",))
    return jax.shard_map(
        per_device,
        mesh=fine,
        in_specs=(
            P(CTX, "tp"),
            P(CTX, "tp"),
            P(CTX, "tp"),
            P(),
            P(None, "tp"),
            P(None, "tp"),
            P(None, "tp"),
            P("tp", CTX),
        ),
        out_specs=(P(CTX, "tp"), P(None, CTX)),
        check_vma=False,
    )
```

```python
import jax
import jax.numpy as jnp
from jax import lax
from jax.experimental import pallas as pl
from jax.experimental.pallas import tpu as pltpu
from jax.sharding import Mesh, PartitionSpec as P

HD = 128
BLK = 128
HEADS = 8
SCALE = HD ** (-0.5)
NEG = -1e30
CTX = ("zh", "zl", "yh", "core")
FAR = (2, 3, 0, 1)
NEAR = (5, 0, 2, 6, 1, 4, 3, 7)
BACK = ((5, 4, 7, 6, 1, 0, 3, 2), (5, 2, 3, 0, 1, 6, 7, 4))
TP = (5, 4, 7, 6, 1, 0, 3, 2)
SLOT = tuple(NEAR.index(j) for j in range(8))
GROUP = ("zl", "yh")
O = 64
MSG = 88
LAST = 80
F32, BF16 = jnp.float32, jnp.bfloat16


def dot_nt(a, b):
    return lax.dot_general(a, b, (((1,), (1,)), ((), ())), preferred_element_type=F32)


def dot_tn(a, b):
    return lax.dot_general(a, b, (((0,), (0,)), ((), ())), preferred_element_type=F32)


def rows_of(shape, dim):
    return lax.broadcasted_iota(jnp.int32, shape, dim)


def split(x):
    high = x.astype(BF16).astype(F32)
    return high, (x - high).astype(BF16).astype(F32)


def position():
    zh, zl, yh, core = (lax.axis_index(a) for a in CTX)
    return zh, zl, yh, core


def heads_class(zh, core):
    return jnp.where(zh == 0, 1 - core, core)


def back_slot(core, j):
    return jnp.where(core == 0, BACK[0].index(j), BACK[1].index(j))


def statistics(m_high, m_low, total):
    t_high, t_low = split(total)
    r = rows_of((8, total.shape[1]), 0)
    zero = jnp.zeros(r.shape, F32)
    out = jnp.where(r == 0, m_high, zero)
    out = jnp.where(r == 1, m_low, out)
    out = jnp.where(r == 2, t_high, out)
    return jnp.where(r == 3, t_low, out)


def column_softmax(scores, mask):
    scores = jnp.where(mask, scores, NEG)
    high, low = split(jnp.max(scores, axis=0, keepdims=True))
    e = jnp.where(mask, jnp.exp(scores - (high + low)), 0.0)
    return high, low, e


def heads_softmax(scores, mask):
    high, low, e = column_softmax(scores, mask)
    return high, low, jnp.sum(e, axis=0, keepdims=True), e.astype(BF16)


def load_kernel(k_ref, v_ref, q_ref, kv_ref, q4_ref, sem):
    zh, zl, yh, core = position()
    first = heads_class(zh, core) * 4
    copies = [
        pltpu.make_async_copy(k_ref, kv_ref.at[0:BLK], sem.at[0]),
        pltpu.make_async_copy(v_ref, kv_ref.at[BLK : 2 * BLK], sem.at[1]),
    ]
    for i in range(4):
        columns = pl.ds(pl.multiple_of((first + i) * HD, HD), HD)
        rows = slice(i * BLK, (i + 1) * BLK)
        copies.append(pltpu.make_async_copy(q_ref.at[:, columns], q4_ref.at[rows], sem.at[2 + i]))
    for c in copies:
        c.start()
    for c in copies:
        c.wait()


def early_kernel(len_ref, q_ref, kv_ref, rk_ref, rv_ref, own_ref, o_ref, st_ref, scratch):
    zh, zl, yh, core = position()
    ctx = ((zh * 4 + zl) * 2 + yh) * 2 + core
    s = dot_nt(kv_ref[0:BLK, :], q_ref[...]) * SCALE
    own = dot_nt(rk_ref[...], q_ref[pl.ds(pl.multiple_of(zl * HD, HD), HD), :]) * SCALE
    high, low, total, e = heads_softmax(s, rows_of(s.shape, 0) < len_ref[ctx])
    o_ref[...] = dot_tn(kv_ref[BLK:, :], e)
    r = rows_of((8, 512), 0)
    st_ref[...] = jnp.where(r == 0, high, jnp.where(r == 1, low, total))
    high, low, total, e = heads_softmax(own, rows_of(own.shape, 0) <= rows_of(own.shape, 1))
    scratch[...] = dot_tn(rv_ref[...], e)
    own_ref[0:O, :] = scratch[pl.ds(pl.multiple_of(yh * O, O), O), :]
    r = rows_of((8, 128), 0)
    own_ref[O : O + 8, :] = jnp.where(r == 0, high + low, total)


def partial_kernel(len_ref, q_ref, kv_ref, sib_ref, own_ref, o_ref, st_ref, out_ref):
    zh, zl, yh, core = position()
    ctx = ((zh * 4 + zl) * 2 + yh) * 2 + core
    s = dot_nt(sib_ref[0:BLK, :], q_ref[...]) * SCALE
    high, low, total, e = heads_softmax(s, rows_of(s.shape, 0) < len_ref[ctx + 1 - 2 * core])
    o = dot_tn(sib_ref[BLK:, :], e)
    high_a, low_a, total_a = st_ref[0:1, :], st_ref[1:2, :], st_ref[2:3, :]
    better = high_a + low_a > high + low
    top_high, top_low = jnp.where(better, high_a, high), jnp.where(better, low_a, low)
    top = top_high + top_low
    wa, wb = jnp.exp(high_a + low_a - top), jnp.exp(high + low - top)
    stats = statistics(top_high, top_low, total_a * wa + total * wb)
    o = o_ref[...] * wa + o * wb
    cls = heads_class(zh, core)
    first = jnp.where(cls == 0, sib_ref[0:BLK, :].astype(F32), kv_ref[BLK:, :].astype(F32))
    for j in range(8):
        cols = slice(j // 2 * HD, (j // 2 + 1) * HD)
        rows = [o[j % 2 * O : (j % 2 + 1) * O, cols], stats[:, cols], first[16 * j : 16 * j + 16]]
        out_ref[SLOT[j]] = jnp.concatenate(rows, axis=0).astype(BF16)


def combine(ref, count, more=()):
    ms, ts, os = [], [], []
    for i in range(count):
        message = ref[i].astype(F32)
        st = message[O : O + 8]
        ms.append((st[0:1], st[1:2]))
        ts.append(st[2:3] + st[3:4])
        os.append(message[0:O])
    high, low = ms[0]
    for h, l in ms[1:]:
        better = h + l > high + low
        high, low = jnp.where(better, h, high), jnp.where(better, l, low)
    top = high + low
    for m, _, _ in more:
        top = jnp.maximum(top, m)
    total = jnp.zeros_like(top)
    summed = jnp.zeros((O, 128), F32)
    for (h, l), t, o in zip(ms, ts, os):
        w = jnp.exp(h + l - top)
        total, summed = total + t * w, summed + o * w
    for m, t, o in more:
        w = jnp.exp(m - top)
        total, summed = total + t * w, summed + o * w
    return high, low, total, summed


def group_kernel(in_ref, out_ref):
    high, low, total, summed = combine(in_ref, 8)
    first = in_ref[SLOT[0]].astype(F32)[O + 8 : MSG]
    message = jnp.concatenate([summed, statistics(high, low, total), first], axis=0).astype(BF16)
    for i in range(4):
        out_ref[i] = message


def final_kernel(in_ref, own_ref, out_ref):
    own = (own_ref[O : O + 1, :], own_ref[O + 1 : O + 2, :], own_ref[0:O, :])
    _, _, total, summed = combine(in_ref, 4, (own,))
    first = in_ref[FAR.index(0)].astype(F32)[O + 8 : MSG]
    message = jnp.concatenate([summed / total, first], axis=0).astype(BF16)
    for i in range(8):
        out_ref[i] = message


def project_kernel(mine_ref, sib_ref, w_ref, out_ref):
    zh, zl, yh, core = position()
    def four(ref, sender, which):
        a = jnp.concatenate([ref[back_slot(sender, j), 0:O, :] for j in range(8)], axis=0)
        return dot_tn(a, w_ref[pl.ds(pl.multiple_of(which * 4 * HD, 4 * HD), 4 * HD), :])

    cls = heads_class(zh, core)
    out = four(mine_ref, core, cls) + four(sib_ref, 1 - core, 1 - cls)
    for i in range(8):
        out_ref[i, :, :] = out.astype(BF16)


def block_kernel(len_ref, q_ref, k_ref, v_ref, mine_ref, sib_ref, out_ref, anchor):
    zh, zl, yh, core = position()
    ctx = ((zh * 4 + zl) * 2 + yh) * 2 + core
    cls = heads_class(zh, core)
    for j in range(8):
        anchor[cls, 16 * j : 16 * j + 16, :] = mine_ref[back_slot(core, j), O:LAST, :]
        anchor[1 - cls, 16 * j : 16 * j + 16, :] = sib_ref[back_slot(1 - core, j), O:LAST, :]
    keys = jnp.concatenate([anchor[0], k_ref[...]], axis=0)
    values = jnp.concatenate([anchor[1], v_ref[...]], axis=0)
    length = len_ref[ctx]
    first = jnp.where(ctx > 0, len_ref[0], 0)
    slot, row = rows_of((BLK, 2 * BLK), 1), rows_of((BLK, 2 * BLK), 0)
    mask = (slot < jnp.minimum(first, BLK)) | (
        (slot >= BLK) & (slot - BLK <= row) & (slot - BLK < length)
    )
    for h in range(HEADS):
        s = dot_nt(q_ref[:, h * HD : (h + 1) * HD], keys) * SCALE
        s = jnp.where(mask, s, NEG)
        e = jnp.where(mask, jnp.exp(s - jnp.max(s, axis=1, keepdims=True)), 0.0)
        total = jnp.sum(e, axis=1, keepdims=True)
        o = jnp.dot(e.astype(BF16), values, preferred_element_type=F32)
        out_ref[:, h * HD : (h + 1) * HD] = (o / total).astype(BF16)


SMEM = pl.BlockSpec(memory_space=pltpu.SMEM)
VMEM = pl.BlockSpec(memory_space=pltpu.VMEM)


def call(kernel, outs, *args, lengths=False, scratch=(), flops=0, space=VMEM):
    specs = ([SMEM] if lengths else []) + [space] * (len(args) - (1 if lengths else 0))
    moved = sum(a.size * a.dtype.itemsize for a in args)
    outs = [jax.ShapeDtypeStruct(shape, dtype) for shape, dtype in outs]
    result = pl.pallas_call(
        kernel,
        out_shape=outs,
        in_specs=specs,
        out_specs=[VMEM] * len(outs),
        scratch_shapes=scratch,
        compiler_params=pltpu.CompilerParams(vmem_limit_bytes=6 << 20),
        cost_estimate=pl.CostEstimate(flops=flops, bytes_accessed=moved, transcendentals=0),
    )(*args)
    return result if len(outs) > 1 else result[0]


def exchange(x, axes, *orders):
    groups = [list(order) for order in orders]
    return lax.all_to_all(x, axes, 0, 0, axis_index_groups=groups, tiled=True)


def carriers(cls):
    return [zh * 2 + (1 - cls if zh == 0 else cls) for zh in FAR]


SWAP = [(0, 1), (1, 0)]


def per_device(bq, bk, bv, lengths, rq, rk, rv, w):
    kv, q4 = call(
        load_kernel, [((2 * BLK, HD), BF16), ((512, HD), BF16)],
        *(pltpu.with_memory_space_constraint(a, pltpu.HBM) for a in (bk, bv, rq)),
        scratch=[pltpu.SemaphoreType.DMA((6,))], space=pl.BlockSpec(memory_space=pltpu.HBM),
    )
    sib = lax.ppermute(kv, "core", SWAP)
    own, o, st = call(
        early_kernel,
        [((O + 8, 128), F32), ((HD, 512), F32), ((8, 512), F32)],
        lengths, q4, kv, rk, rv, lengths=True, scratch=[pltpu.VMEM((HD, 128), F32)],
    )
    parts = call(
        partial_kernel, [((8, MSG, 128), BF16)], lengths, q4, kv, sib, own, o, st, lengths=True
    )
    parts = exchange(parts, GROUP, NEAR)
    grouped = call(group_kernel, [((4, MSG, 128), BF16)], parts)
    grouped = exchange(grouped, ("zh", "core"), carriers(0), carriers(1))
    attn = call(final_kernel, [((8, LAST, 128), BF16)], grouped, own)
    attn = exchange(attn, GROUP + ("core",), *[[2 * j + c for j in BACK[c]] for c in range(2)])
    attn_sib = lax.ppermute(attn, "core", SWAP)
    partial = call(project_kernel, [((8, 128, 128), BF16)], attn, attn_sib, w)
    partial = exchange(partial, "tp", TP)
    row_output = jnp.sum(partial.astype(F32), axis=0)
    block_attention = call(
        block_kernel, [(bq.shape, BF16)], lengths, bq, bk, bv, attn, attn_sib,
        lengths=True, scratch=[pltpu.VMEM((2, BLK, HD), BF16)],
    )
    return block_attention, row_output


def solution(mesh):
    fine = Mesh(mesh.devices.reshape(4, 4, 2, 2, 8), CTX + ("tp",))
    return jax.shard_map(
        per_device,
        mesh=fine,
        in_specs=(
            P(CTX, "tp"),
            P(CTX, "tp"),
            P(CTX, "tp"),
            P(),
            P(None, "tp"),
            P(None, "tp"),
            P(None, "tp"),
            P("tp", CTX),
        ),
        out_specs=(P(CTX, "tp"), P(None, CTX)),
        check_vma=False,
    )
```
